32 devices in a mesh: groups: 1, ex: 32 (over z, y, x, core).
Axes of the slice: x: 2, y: 2, z: 4, core: 2. Of those that a mesh axis runs over, the one named last changes fastest.
Arguments:
- tokens: bfloat16 [2048, 2880], P(('groups', 'ex')), may hold values from -6 to 6
- norm_gain: float32 [2880], replicated, may hold values from 0.5 to 1.5
- expert_ids: int32 [2048, 4], P(('groups', 'ex')), may hold values from 0 to 7, all different within a row; in each aligned block of 64 rows (0 to 63, 64 to 127, ...) at most 48 rows name the same one
- gate_weights: float32 [2048, 4], P(('groups', 'ex')), may hold values from 0.05 to 0.6
- gate_proj: bfloat16 [32, 2880, 640], P('ex'), may hold values from -0.109375 to 0.109375
- up_proj: bfloat16 [32, 2880, 640], P('ex'), may hold values from -0.109375 to 0.109375
- down_proj: bfloat16 [32, 640, 2880], P('ex'), may hold values from -0.125 to 0.125
Outputs:
- mixed: bfloat16 [2048, 2880], P(('groups', 'ex'))
The draws below stay inside these ranges and needn't reach their ends.
Inputs may be any that keep to these rules, and one draw needn't show every extreme that they name: `expert_ids`: each row names 4 different experts. In each aligned block of 64 rows (the rows of one index of ex) no expert is named by more than 48 rows, a bound that some block reaches.
All inputs are finite; a program needn't handle non-finite values.
Results may differ from the reference program's by a relative error of at most 0.0065.
Values may be sent and summed in bfloat16 or wider, within the bound.
No kernel may reach another device: no remote copies, remote signals or barrier semaphores. Data moves between devices by JAX's collectives and lax.ppermute only.
A program may use at most 128 MiB of HBM per device.

```python
import math
import jax
import jax.numpy as jnp
import numpy as np
from jax import lax

D = 2880
TOP = 4
SLICES = 4
HID_DEV = 640
TOK_DEV = 64
EXPERTS = 8
HID = 2560
CAP = 48
TOKENS = 2048


def block_levels(stream_key, extent, cuts, least, high):
    gain = 1.0
    for axis_at, blocks in cuts:
        draws = jax.random.uniform(jax.random.fold_in(jax.random.fold_in(stream_key, 6), axis_at), (blocks,), jnp.float32, least / len(cuts), high / len(cuts))
        gain = gain * jnp.repeat(jnp.exp(draws), extent[axis_at] // blocks).reshape((-1,) + (1,) * (len(extent) - 1 - axis_at))
    return gain


def deal_out(rng, own, number, rows, amount, top, bound, lean):
    ranking = jax.random.permutation(rng, amount)
    crowded, usual = portions_of(amount, rows * top, bound, lean, True), portions_of(amount, rows * top, bound, lean, False)
    places = jnp.arange(amount)

    def named(tallies, turn):
        used = int((tallies > 0).sum())
        fixed = max(1, used // 4)
        passed = fixed + (places - fixed + turn * (used - fixed)) % max(1, amount - fixed)
        return jnp.zeros((amount,), jnp.int32).at[ranking[jnp.where(places < fixed, places, passed)]].set(jnp.asarray(tallies, jnp.int32))

    tallies = jnp.where(number % 4 == 0, named(crowded, number // 4), named(usual, number - number // 4 - 1))
    mixed = jax.random.permutation(jax.random.fold_in(own, 3), amount)
    donor, sink = mixed[0:amount // 2 * 2:2], mixed[1:amount // 2 * 2:2]
    margin = jnp.minimum(tallies[donor] - 1, bound - tallies[sink]) // 2
    margin = jnp.where((donor == ranking[0]) | (sink == ranking[0]) | (tallies[sink] == 0), 0, jnp.maximum(margin, 0))
    passed = jax.random.randint(jax.random.fold_in(own, 4), (amount // 2,), 0, 1 << 20) % (margin + 1)
    tallies = tallies.at[donor].add(-passed).at[sink].add(passed)
    labels = jnp.searchsorted(jnp.cumsum(tallies), jnp.arange(rows * top), side="right").astype(jnp.int32)
    table = labels.reshape(top, rows).T
    table = table[jax.random.permutation(jax.random.fold_in(own, 1), rows)]
    turn = jax.random.randint(jax.random.fold_in(own, 2), (rows, 1), 0, top)
    return jnp.take_along_axis(table, (jnp.arange(top)[None, :] + turn) % top, axis=1)


def portions_of(count, total, reach, slope, full):
    portions = [(1 << 20) // math.isqrt(grade ** slope) + 1 for grade in range(1, count + 1)]
    largest = reach if full else min(reach, max(-(-total // count), total * portions[0] // sum(portions)))
    least = 1 if total - largest >= count - 1 else 0
    counts, surplus = [largest] + [least] * (count - 1), total - largest - least * (count - 1)
    while surplus > 0:
        free = [i for i in range(1, count) if counts[i] < largest] or [i for i in range(1, count) if counts[i] < reach]
        mass, remaining = sum([portions[i] for i in free]), surplus
        for i in free:
            more = min(reach - counts[i], max(1, remaining * portions[i] // mass), surplus)
            counts[i] = counts[i] + more
            surplus = surplus - more
    return np.array(counts)


def centred(key, shape, scale, reach, split=(), kind=jnp.bfloat16):
    values = scale * jax.random.normal(key, shape, jnp.float32)
    if split:
        values = values * block_levels(key, shape, split, -0.22, 0.18)
    return jnp.clip(values, -reach, reach).astype(kind)


def setup_inputs(seed: int = 0, part: int = 0) -> dict:
    arg_keys = jax.random.split(jax.random.key(seed), 8)
    own_keys = jax.random.split(jax.random.fold_in(arg_keys[7], part), 8)
    tokens = centred(own_keys[0], (TOKENS, D), 1.0, 6.0, ((0, 32),))
    norm_gain = jnp.clip(1.0 + 0.1 * jax.random.normal(arg_keys[1], (D,), jnp.float32), 0.5, 1.5)
    expert_ids_keys = jax.random.split(jax.random.fold_in(own_keys[2], 1), TOKENS // TOK_DEV)
    expert_ids_turns = jax.random.permutation(jax.random.fold_in(own_keys[2], 3), TOKENS // TOK_DEV)
    expert_ids = jax.vmap(lambda own, number: deal_out(jax.random.fold_in(own_keys[2], 2), own, number, TOK_DEV, EXPERTS, TOP, CAP, 1))(expert_ids_keys, expert_ids_turns).reshape((TOKENS, TOP))
    gate_weights = jnp.clip(0.05 + 0.55 * jax.random.uniform(own_keys[3], (TOKENS, TOP), jnp.float32) ** block_levels(own_keys[3], (TOKENS, TOP), ((0, 32),), -0.2, 0.2), 0.05, 0.6)
    gate_proj = centred(arg_keys[4], (SLICES * EXPERTS, D, HID_DEV), D ** -0.5, 0.109375, ((0, 32),))
    up_proj = centred(arg_keys[5], (SLICES * EXPERTS, D, HID_DEV), D ** -0.5, 0.109375, ((0, 32),))
    down_proj = centred(arg_keys[6], (SLICES * EXPERTS, HID_DEV, D), HID ** -0.5, 0.125, ((0, 32),))
    return dict(tokens=tokens, norm_gain=norm_gain, expert_ids=expert_ids, gate_weights=gate_weights, gate_proj=gate_proj, up_proj=up_proj, down_proj=down_proj)


def reference(tokens, norm_gain, expert_ids, gate_weights, gate_proj, up_proj, down_proj):
    values = tokens.astype(jnp.float32)
    mean_sq = lax.optimization_barrier(jnp.mean(values * values, axis=-1, keepdims=True))
    normed = (values * lax.rsqrt(mean_sq + 1e-05) * norm_gain).astype(jnp.bfloat16)
    blocks = TOKENS // TOK_DEV
    chosen = expert_ids.reshape(blocks, TOK_DEV * TOP)
    onehot = (chosen[:, :, None] == jnp.arange(EXPERTS, dtype=jnp.int32)[None, None, :]).astype(jnp.int32)
    before = jnp.cumsum(onehot, axis=1) - onehot
    rank_in = lax.optimization_barrier(jnp.sum(before * onehot, axis=-1)).astype(jnp.int32)
    slot_index = (jnp.arange(blocks, dtype=jnp.int32)[:, None] * CAP + rank_in).reshape(-1).astype(jnp.int32)
    flat_expert = chosen.reshape(-1).astype(jnp.int32)
    token_index = (jnp.arange(TOKENS * TOP, dtype=jnp.int32) // TOP).astype(jnp.int32)
    table = jnp.full((EXPERTS, blocks * CAP), TOKENS, jnp.int32).at[flat_expert, slot_index].set(token_index)
    weight_table = jnp.zeros((EXPERTS, blocks * CAP), jnp.float32).at[flat_expert, slot_index].set(gate_weights.reshape(-1))
    padded = jnp.concatenate([normed, jnp.zeros((1, D), normed.dtype)], axis=0)
    gate_full = gate_proj.reshape(SLICES, EXPERTS, D, HID_DEV).transpose(1, 2, 0, 3).reshape(EXPERTS, D, HID)
    up_full = up_proj.reshape(SLICES, EXPERTS, D, HID_DEV).transpose(1, 2, 0, 3).reshape(EXPERTS, D, HID)
    down_full = down_proj.reshape(SLICES, EXPERTS, HID_DEV, D).transpose(1, 0, 2, 3).reshape(EXPERTS, HID, D)

    def one_expert(carry, pieces):
        rows_index, row_weights, gate_w, up_w, down_w = pieces
        routed = padded[rows_index]
        gate_act = jnp.dot(routed, gate_w, preferred_element_type=jnp.float32)
        up_act = jnp.dot(routed, up_w, preferred_element_type=jnp.float32)
        hidden = (jax.nn.silu(gate_act) * up_act).astype(jnp.bfloat16)
        produced = jnp.dot(hidden, down_w, preferred_element_type=jnp.float32)
        carry = carry.at[rows_index].add(row_weights[:, None] * produced)
        return (carry, None)
    start = jnp.zeros((TOKENS + 1, D), jnp.float32)
    summed, unused = lax.scan(one_expert, start, (table, weight_table, gate_full, up_full, down_full))
    return summed[:TOKENS].astype(jnp.bfloat16)
```

```python
import jax
import jax.numpy as jnp
from jax import lax
from jax.sharding import PartitionSpec as P

SLICES = 4
LANES = 128
BF16 = jnp.bfloat16
F32 = jnp.float32


def normalise(tokens, norm_gain):
    values = tokens.astype(F32)
    mean_sq = jnp.mean(values * values, axis=-1, keepdims=True)
    return (values * lax.rsqrt(mean_sq + 1e-05) * norm_gain).astype(BF16)


def expert_rows(flat_rows, gate_w, up_w, down_w):
    gate_act = jnp.dot(flat_rows, gate_w, preferred_element_type=F32)
    up_act = jnp.dot(flat_rows, up_w, preferred_element_type=F32)
    hidden = (jax.nn.silu(gate_act) * up_act).astype(BF16)
    return jnp.dot(hidden, down_w, preferred_element_type=F32)


def local_general(tokens, norm_gain, expert_ids, gate_weights, gate_proj, up_proj, down_proj):
    tok_rows, features = tokens.shape
    picks = expert_ids.shape[1]
    devices = lax.axis_size("ex")
    experts = devices // SLICES
    capacity = min(tok_rows, 4 * ((3 * tok_rows * picks + 8 * experts - 1) // (8 * experts)))
    normed = normalise(tokens, norm_gain)
    padded = jnp.concatenate([normed, jnp.zeros((1, features), normed.dtype)], axis=0)
    flat_expert = expert_ids.reshape(-1)
    onehot = (flat_expert[:, None] == jnp.arange(experts, dtype=jnp.int32)[None, :]).astype(
        jnp.int32
    )
    before = jnp.cumsum(onehot, axis=0) - onehot
    rank_in = jnp.sum(before * onehot, axis=1)
    token_index = jnp.arange(tok_rows * picks, dtype=jnp.int32) // picks
    slot_index = flat_expert * capacity + rank_in
    table = jnp.full((experts * capacity,), tok_rows, jnp.int32).at[slot_index].set(token_index)
    buffer = padded[table].reshape(experts, capacity, features)
    outgoing = jnp.tile(buffer, (SLICES, 1, 1))
    arrived = lax.all_to_all(outgoing, "ex", split_axis=0, concat_axis=0, tiled=True)
    partials = expert_rows(arrived.reshape(-1, features), gate_proj[0], up_proj[0], down_proj[0])
    partials = partials.reshape(devices, capacity, features)
    returned = lax.all_to_all(partials, "ex", split_axis=0, concat_axis=0, tiled=True)
    summed = jnp.sum(returned.reshape(SLICES, experts * capacity, features), axis=0)
    gathered = summed[slot_index].reshape(tok_rows, picks, features)
    mixed = jnp.sum(gathered * gate_weights[:, :, None], axis=1)
    return mixed.astype(BF16)


def local_cube(tokens, norm_gain, expert_ids, gate_weights, gate_proj, up_proj, down_proj):
    tok_rows, features = tokens.shape
    devices = lax.axis_size("ex")
    experts = devices // SLICES
    mine = lax.axis_index("ex") % experts
    width = -(-(features + 3 * experts) // LANES) * LANES

    def swap(array, partner):
        return lax.ppermute(array, "ex", [(i, partner(i)) for i in range(devices)])

    def first(i):
        return i ^ (2 if i % 2 == 0 else 4)

    def second(i):
        return i ^ (4 if i % 2 == 0 else 2)

    def core(i):
        return i ^ 1

    def slice_bits(j):
        return lambda i: i ^ (j * experts)

    normed = normalise(tokens, norm_gain)
    picked = expert_ids[:, :, None] == jnp.arange(experts, dtype=jnp.int32)[None, None, :]
    dense = jnp.sum(jnp.where(picked, gate_weights[:, :, None], 0.0), axis=1)
    high = lax.reduce_precision(dense, 8, 7)
    rest = dense - high
    middle = lax.reduce_precision(rest, 8, 7)
    low = rest - middle
    extra = [part.astype(BF16) for part in (high, middle, low)]
    fill = jnp.zeros((tok_rows, width - features - 3 * experts), BF16)
    rows = jnp.concatenate([normed, *extra, fill], axis=1)

    def partial(block):
        produced = expert_rows(block[:, :features], gate_proj[0], up_proj[0], down_proj[0])
        parts = block[:, features : features + 3 * experts].astype(F32)
        column = jnp.arange(3 * experts, dtype=jnp.int32) % experts == mine
        weight = jnp.sum(jnp.where(column[None, :], parts, 0.0), axis=1, keepdims=True)
        return produced * weight

    blocks = [rows] + [swap(rows, slice_bits(j)) for j in range(1, SLICES)]
    total = None
    for j, block in enumerate(blocks):
        half = jnp.concatenate([block, swap(block, first)], axis=0)
        full = jnp.concatenate([half, swap(half, second)], axis=0)
        other = swap(full, core)
        back = swap(partial(other).astype(BF16), core)
        sums = partial(full) + back.astype(F32)
        cut = 2 * tok_rows
        sums = sums[:cut] + swap(sums[cut:].astype(BF16), second).astype(F32)
        sums = sums[:tok_rows] + swap(sums[tok_rows:].astype(BF16), first).astype(F32)
        if j:
            sums = swap(sums.astype(BF16), slice_bits(j)).astype(F32)
        total = sums if total is None else total + sums
    return total.astype(BF16)


def solution(mesh):
    in_specs = (
        P(("groups", "ex"), None),
        P(),
        P(("groups", "ex"), None),
        P(("groups", "ex"), None),
        P("ex", None, None),
        P("ex", None, None),
        P("ex", None, None),
    )
    out_specs = P(("groups", "ex"), None)
    local = local_cube if mesh.shape["ex"] == 8 * SLICES else local_general
    return jax.shard_map(local, mesh=mesh, in_specs=in_specs, out_specs=out_specs, check_vma=False)
```

```python
import functools

import jax
import jax.numpy as jnp
from jax import lax
from jax.experimental import pallas as pl
from jax.experimental.pallas import tpu as pltpu
from jax.sharding import PartitionSpec as P

SLICES = 4
LANES = 128
BF16 = jnp.bfloat16
F32 = jnp.float32


def normalise(tokens, norm_gain):
    values = tokens.astype(F32)
    mean_sq = jnp.mean(values * values, axis=-1, keepdims=True)
    return (values * lax.rsqrt(mean_sq + 1e-05) * norm_gain).astype(BF16)


def expert_rows(flat_rows, gate_w, up_w, down_w):
    gate_act = jnp.dot(flat_rows, gate_w, preferred_element_type=F32)
    up_act = jnp.dot(flat_rows, up_w, preferred_element_type=F32)
    hidden = (jax.nn.silu(gate_act) * up_act).astype(BF16)
    return jnp.dot(hidden, down_w, preferred_element_type=F32)


def local_general(tokens, norm_gain, expert_ids, gate_weights, gate_proj, up_proj, down_proj):
    tok_rows, features = tokens.shape
    picks = expert_ids.shape[1]
    devices = lax.axis_size("ex")
    experts = devices // SLICES
    capacity = min(tok_rows, 4 * ((3 * tok_rows * picks + 8 * experts - 1) // (8 * experts)))
    normed = normalise(tokens, norm_gain)
    padded = jnp.concatenate([normed, jnp.zeros((1, features), normed.dtype)], axis=0)
    flat_expert = expert_ids.reshape(-1)
    onehot = (flat_expert[:, None] == jnp.arange(experts, dtype=jnp.int32)[None, :]).astype(
        jnp.int32
    )
    before = jnp.cumsum(onehot, axis=0) - onehot
    rank_in = jnp.sum(before * onehot, axis=1)
    token_index = jnp.arange(tok_rows * picks, dtype=jnp.int32) // picks
    slot_index = flat_expert * capacity + rank_in
    table = jnp.full((experts * capacity,), tok_rows, jnp.int32).at[slot_index].set(token_index)
    buffer = padded[table].reshape(experts, capacity, features)
    outgoing = jnp.tile(buffer, (SLICES, 1, 1))
    arrived = lax.all_to_all(outgoing, "ex", split_axis=0, concat_axis=0, tiled=True)
    partials = expert_rows(arrived.reshape(-1, features), gate_proj[0], up_proj[0], down_proj[0])
    partials = partials.reshape(devices, capacity, features)
    returned = lax.all_to_all(partials, "ex", split_axis=0, concat_axis=0, tiled=True)
    summed = jnp.sum(returned.reshape(SLICES, experts * capacity, features), axis=0)
    gathered = summed[slot_index].reshape(tok_rows, picks, features)
    mixed = jnp.sum(gathered * gate_weights[:, :, None], axis=1)
    return mixed.astype(BF16)


def pieces(extent, size):
    return [(at, min(size, extent - at)) for at in range(0, extent, size)]


def load_kernel(*refs):
    count = len(refs) // 3
    copies = [
        pltpu.make_async_copy(refs[n].at[0], refs[count + n], refs[2 * count + n]) for n in range(count)
    ]
    for copy in copies:
        copy.start()
    for copy in copies:
        copy.wait()


def load_call(*arrays):
    count = len(arrays)
    return pl.pallas_call(
        load_kernel,
        out_shape=tuple(pltpu.VMEM(a.shape[1:], a.dtype) for a in arrays),
        in_specs=[pl.BlockSpec(memory_space=pl.ANY)] * count,
        out_specs=(pl.BlockSpec(memory_space=pltpu.VMEM),) * count,
        scratch_shapes=[pltpu.SemaphoreType.DMA] * count,
        compiler_params=pltpu.CompilerParams(vmem_limit_bytes=16 * 2**20),
    )(*arrays)


def rows_kernel(experts, tokens_ref, gain_ref, ids_ref, weights_ref, rows_ref):
    tok_rows, features = tokens_ref.shape
    values = tokens_ref[...].astype(F32)
    mean_sq = jnp.sum(values * values, axis=-1, keepdims=True) * (1.0 / features)
    rows_ref[:, :features] = (values * lax.rsqrt(mean_sq + 1e-05) * gain_ref[...]).astype(BF16)
    lane = lax.broadcasted_iota(jnp.int32, (tok_rows, rows_ref.shape[1] - features), 1)
    expert = lax.rem(lane, experts)
    ids, chosen = ids_ref[...], weights_ref[...]
    dense = jnp.zeros(lane.shape, F32)
    for j in range(ids.shape[1]):
        dense += jnp.where(expert == ids[:, j : j + 1], chosen[:, j : j + 1], 0.0)
    high = dense.astype(BF16).astype(F32)
    middle = (dense - high).astype(BF16).astype(F32)
    low = dense - high - middle
    term = jnp.where(lane < experts, high, jnp.where(lane < 2 * experts, middle, low))
    rows_ref[:, features:] = jnp.where(lane < 3 * experts, term, 0.0).astype(BF16)


def rows_call(tokens, norm_gain, expert_ids, gate_weights, experts, width):
    return pl.pallas_call(
        functools.partial(rows_kernel, experts),
        out_shape=jax.ShapeDtypeStruct((tokens.shape[0], width), BF16),
        in_specs=[pl.BlockSpec(memory_space=pltpu.VMEM)] * 4,
        out_specs=pl.BlockSpec(memory_space=pltpu.VMEM),
        compiler_params=pltpu.CompilerParams(vmem_limit_bytes=16 * 2**20),
    )(tokens, norm_gain[None, :], expert_ids, gate_weights)


def expert_kernel(x_ref, mask_ref, gate_ref, up_ref, down_ref, y_ref, hidden_ref):
    features, hidden = gate_ref.shape
    for at, size in pieces(hidden, 2 * LANES):
        gate = jnp.dot(x_ref[:, :features], gate_ref[:, at : at + size], preferred_element_type=F32)
        up = jnp.dot(x_ref[:, :features], up_ref[:, at : at + size], preferred_element_type=F32)
        hidden_ref[:, at : at + size] = (gate * jax.nn.sigmoid(gate) * up).astype(BF16)
    tail = features // LANES * LANES
    parts = x_ref[:, tail : tail + LANES].astype(F32)
    weight = jnp.sum(jnp.where(mask_ref[...] > 0.0, parts, 0.0), axis=1, keepdims=True)
    for at, size in pieces(features, 6 * LANES):
        y = lax.dot_general(
            hidden_ref[...],
            down_ref[at : at + size, :],
            (((1,), (1,)), ((), ())),
            preferred_element_type=F32,
        )
        y_ref[:, at : at + size] = (y * weight).astype(BF16)
    y_ref[:, features:] = jnp.zeros((y_ref.shape[0], y_ref.shape[1] - features), BF16)


def expert_call(x, mask, gate_w, up_w, down_t):
    rows = x.shape[0]
    features, hidden = gate_w.shape
    return pl.pallas_call(
        expert_kernel,
        out_shape=jax.ShapeDtypeStruct(x.shape, BF16),
        in_specs=[pl.BlockSpec(memory_space=pltpu.VMEM)] * 5,
        out_specs=pl.BlockSpec(memory_space=pltpu.VMEM),
        scratch_shapes=[pltpu.VMEM((rows, hidden), BF16)],
        compiler_params=pltpu.CompilerParams(vmem_limit_bytes=16 * 2**20),
        cost_estimate=pl.CostEstimate(
            flops=6 * rows * features * hidden, bytes_accessed=4 * rows * features, transcendentals=0
        ),
    )(x, mask, gate_w, up_w, down_t)


def local_cube(tokens, norm_gain, expert_ids, gate_weights, gate_proj, up_proj, down_proj):
    tok_rows, features = tokens.shape
    devices = lax.axis_size("ex")
    experts = devices // SLICES
    mine = lax.axis_index("ex") % experts
    width = -(-(features + 3 * experts) // LANES) * LANES

    def swap(array, partner):
        return lax.ppermute(array, "ex", [(i, partner(i)) for i in range(devices)])

    def first(i):
        return i ^ (2 if i % 2 == 0 else 4)

    def second(i):
        return i ^ (4 if i % 2 == 0 else 2)

    def core(i):
        return i ^ 1

    def slice_bits(j):
        return lambda i: i ^ (j * experts)

    rows = rows_call(tokens, norm_gain, expert_ids, gate_weights, experts, width)
    lane = jnp.arange(LANES, dtype=jnp.int32)[None, :] - features % LANES
    mask = ((lane >= 0) & (lane < 3 * experts) & (lane % experts == mine)).astype(F32)
    stored = (gate_proj, up_proj, jnp.swapaxes(down_proj, 1, 2))
    loaded = load_call(*(pltpu.with_memory_space_constraint(w, pltpu.HBM) for w in stored))
    weights = [pltpu.with_memory_space_constraint(w, pltpu.VMEM) for w in loaded]

    last = [mask]

    def order(value):
        value = lax.optimization_barrier((value, last[0]))[0]
        last[0] = value
        return value

    def expert(x):
        y = expert_call(x, mask, *weights)
        last[0] = y
        return y

    def add(a, b):
        return (a.astype(F32) + b.astype(F32)).astype(BF16)

    cut = 2 * tok_rows
    p1, p2, half, full, c, own, back, q2, q1, z, zb = ([None] * SLICES for _ in range(11))

    def gather_half(j, block):
        half[j] = jnp.concatenate([block, order(p1[j])], axis=0)
        p2[j] = swap(half[j], second)

    def gather_full(j):
        full[j] = jnp.concatenate([half[j], order(p2[j])], axis=0)
        c[j] = swap(full[j], core)

    def run_own(j):
        own[j] = expert(order(full[j]))

    def run_other(j):
        back[j] = swap(expert(order(c[j])), core)

    def reduce_core(j):
        arrived = order(back[j])
        q2[j] = swap(add(own[j][cut:], arrived[cut:]), second)
        own[j] = add(own[j][:cut], arrived[:cut])

    def reduce_second(j):
        arrived = order(q2[j])
        q1[j] = swap(add(own[j][tok_rows:], arrived[tok_rows:]), first)
        own[j] = add(own[j][:tok_rows], arrived[:tok_rows])

    def reduce_first(j):
        sums = add(own[j], order(q1[j]))
        zb[j] = swap(sums, slice_bits(j)) if j else sums

    p1[0] = swap(rows, first)
    z[1] = order(swap(rows, slice_bits(1)))
    gather_half(0, rows)
    z[2] = swap(order(rows), slice_bits(2))
    p1[1] = swap(z[1], first)
    gather_full(0)
    gather_half(1, z[1])
    run_own(0)
    z[2] = order(z[2])
    p1[2] = swap(z[2], first)
    z[3] = swap(order(rows), slice_bits(3))
    run_other(0)
    gather_full(1)
    gather_half(2, z[2])
    run_own(1)
    run_other(1)
    reduce_core(0)
    gather_full(2)
    z[3] = order(z[3])
    p1[3] = swap(z[3], first)
    run_own(2)
    run_other(2)
    gather_half(3, z[3])
    reduce_core(1)
    reduce_second(0)
    gather_full(3)
    run_own(3)
    run_other(3)
    reduce_core(2)
    reduce_second(1)
    reduce_core(3)
    reduce_first(1)
    reduce_second(2)
    reduce_first(2)
    reduce_second(3)
    reduce_first(3)
    reduce_first(0)
    total = sum(order(zb[j]).astype(F32) for j in range(SLICES))
    return total[:, :features].astype(BF16)


def solution(mesh):
    in_specs = (
        P(("groups", "ex"), None),
        P(),
        P(("groups", "ex"), None),
        P(("groups", "ex"), None),
        P("ex", None, None),
        P("ex", None, None),
        P("ex", None, None),
    )
    out_specs = P(("groups", "ex"), None)
    local = local_cube if mesh.shape["ex"] == 8 * SLICES else local_general
    return jax.shard_map(local, mesh=mesh, in_specs=in_specs, out_specs=out_specs, check_vma=False)
```

```python
import functools

import jax
import jax.numpy as jnp
from jax import lax
from jax.experimental import pallas as pl
from jax.experimental.pallas import tpu as pltpu
from jax.sharding import PartitionSpec as P

SLICES = 4
LANES = 128
UNITS = 2 * LANES
COLUMNS = 6 * LANES
BF16 = jnp.bfloat16
F32 = jnp.float32


def normalise(tokens, norm_gain):
    values = tokens.astype(F32)
    mean_sq = jnp.mean(values * values, axis=-1, keepdims=True)
    return (values * lax.rsqrt(mean_sq + 1e-05) * norm_gain).astype(BF16)


def expert_rows(flat_rows, gate_w, up_w, down_w):
    gate_act = jnp.dot(flat_rows, gate_w, preferred_element_type=F32)
    up_act = jnp.dot(flat_rows, up_w, preferred_element_type=F32)
    hidden = (jax.nn.silu(gate_act) * up_act).astype(BF16)
    return jnp.dot(hidden, down_w, preferred_element_type=F32)


def local_general(tokens, norm_gain, expert_ids, gate_weights, gate_proj, up_proj, down_proj):
    tok_rows, features = tokens.shape
    picks = expert_ids.shape[1]
    devices = lax.axis_size("ex")
    experts = devices // SLICES
    capacity = min(tok_rows, 4 * ((3 * tok_rows * picks + 8 * experts - 1) // (8 * experts)))
    normed = normalise(tokens, norm_gain)
    padded = jnp.concatenate([normed, jnp.zeros((1, features), normed.dtype)], axis=0)
    flat_expert = expert_ids.reshape(-1)
    onehot = (flat_expert[:, None] == jnp.arange(experts, dtype=jnp.int32)[None, :]).astype(
        jnp.int32
    )
    before = jnp.cumsum(onehot, axis=0) - onehot
    rank_in = jnp.sum(before * onehot, axis=1)
    token_index = jnp.arange(tok_rows * picks, dtype=jnp.int32) // picks
    slot_index = flat_expert * capacity + rank_in
    table = jnp.full((experts * capacity,), tok_rows, jnp.int32).at[slot_index].set(token_index)
    buffer = padded[table].reshape(experts, capacity, features)
    outgoing = jnp.tile(buffer, (SLICES, 1, 1))
    arrived = lax.all_to_all(outgoing, "ex", split_axis=0, concat_axis=0, tiled=True)
    partials = expert_rows(arrived.reshape(-1, features), gate_proj[0], up_proj[0], down_proj[0])
    partials = partials.reshape(devices, capacity, features)
    returned = lax.all_to_all(partials, "ex", split_axis=0, concat_axis=0, tiled=True)
    summed = jnp.sum(returned.reshape(SLICES, experts * capacity, features), axis=0)
    gathered = summed[slot_index].reshape(tok_rows, picks, features)
    mixed = jnp.sum(gathered * gate_weights[:, :, None], axis=1)
    return mixed.astype(BF16)


def pieces(extent, size):
    return [(at, min(size, extent - at)) for at in range(0, extent, size)]


def rows_kernel(
    experts, tokens_any, gain_any, ids_any, weights_any, rows_ref, tokens_ref, gain_ref, ids_ref, weights_ref, sems
):
    copies = [
        pltpu.make_async_copy(tokens_any, tokens_ref, sems.at[0]),
        pltpu.make_async_copy(gain_any, gain_ref, sems.at[1]),
        pltpu.make_async_copy(ids_any, ids_ref, sems.at[2]),
        pltpu.make_async_copy(weights_any, weights_ref, sems.at[3]),
    ]
    for copy in copies:
        copy.start()
    for copy in copies:
        copy.wait()
    tok_rows, features = tokens_ref.shape
    extra = rows_ref.shape[1] - features
    values = tokens_ref[...].astype(F32)
    mean_sq = jnp.sum(values * values, axis=-1, keepdims=True) * (1.0 / features)
    rows_ref[:, :features] = (values * lax.rsqrt(mean_sq + 1e-05) * gain_ref[...][None, :]).astype(BF16)
    place = lax.broadcasted_iota(jnp.int32, (extra, tok_rows), 0)
    expert = lax.rem(place, experts)
    dense = jnp.zeros((extra, tok_rows), F32)
    for j in range(ids_ref.shape[0]):
        dense += jnp.where(expert == ids_ref[j : j + 1, :], weights_ref[j : j + 1, :], 0.0)
    high = dense.astype(BF16).astype(F32)
    middle = (dense - high).astype(BF16).astype(F32)
    low = dense - high - middle
    term = jnp.where(place < experts, high, jnp.where(place < 2 * experts, middle, low))
    term = jnp.where(place < 3 * experts, term, 0.0).astype(BF16)
    row = lax.broadcasted_iota(jnp.int32, (extra, extra), 0)
    column = lax.broadcasted_iota(jnp.int32, (extra, extra), 1)
    unit = jnp.where(row == column, 1.0, 0.0).astype(BF16)
    turned = lax.dot_general(term, unit, (((0,), (0,)), ((), ())), preferred_element_type=F32)
    rows_ref[:, features:] = turned.astype(BF16)


def rows_call(tokens, norm_gain, expert_ids, gate_weights, experts, width):
    arrays = (tokens, norm_gain, jnp.swapaxes(expert_ids, 0, 1), jnp.swapaxes(gate_weights, 0, 1))
    return pl.pallas_call(
        functools.partial(rows_kernel, experts),
        out_shape=jax.ShapeDtypeStruct((tokens.shape[0], width), BF16),
        in_specs=[pl.BlockSpec(memory_space=pl.ANY)] * 4,
        out_specs=pl.BlockSpec(memory_space=pltpu.VMEM),
        scratch_shapes=[pltpu.VMEM(a.shape, a.dtype) for a in arrays] + [pltpu.SemaphoreType.DMA((4,))],
        compiler_params=pltpu.CompilerParams(vmem_limit_bytes=16 * 2**20),
    )(*(pltpu.with_memory_space_constraint(a, pltpu.HBM) for a in arrays))


def expert_body(xa_ref, xb_ref, mask_ref, gate_ref, up_ref, down_ref, ya_ref, yb_ref, x_ref, hidden_ref, ready):
    features, hidden = gate_ref.shape
    rows = xa_ref.shape[0]
    x_ref[:rows, :] = xa_ref[...]
    x_ref[rows:, :] = xb_ref[...]
    for n, (at, size) in enumerate(pieces(hidden, UNITS)):
        ready(0, n)
        gate = jnp.dot(x_ref[:, :features], gate_ref[:, at : at + size], preferred_element_type=F32)
        up = jnp.dot(x_ref[:, :features], up_ref[:, at : at + size], preferred_element_type=F32)
        hidden_ref[:, at : at + size] = (gate * jax.nn.sigmoid(gate) * up).astype(BF16)
    tail = features // LANES * LANES
    parts = x_ref[:, tail : tail + LANES].astype(F32)
    weight = jnp.sum(jnp.where(mask_ref[...] > 0.0, parts, 0.0), axis=1, keepdims=True)
    for n, (at, size) in enumerate(pieces(features, COLUMNS)):
        ready(1, n)
        y = lax.dot_general(
            hidden_ref[...],
            down_ref[at : at + size, :],
            (((1,), (1,)), ((), ())),
            preferred_element_type=F32,
        )
        y = (y * weight).astype(BF16)
        ya_ref[:, at : at + size] = y[:rows]
        yb_ref[:, at : at + size] = y[rows:]
    blank = jnp.zeros((rows, ya_ref.shape[1] - features), BF16)
    ya_ref[:, features:] = blank
    yb_ref[:, features:] = blank


def expert_kernel(xa, xb, mask, gate, up, down, ya, yb, x, hidden):
    expert_body(xa, xb, mask, gate, up, down, ya, yb, x, hidden, lambda part, n: None)


def first_kernel(xa, xb, mask, gate_any, up_any, down_any, ya, yb, gate, up, down, x, hidden, sems_wide, sems_down):
    wide = []
    for n, (at, size) in enumerate(pieces(gate.shape[1], UNITS)):
        cut = pl.ds(at, size)
        wide.append(
            [
                pltpu.make_async_copy(gate_any.at[0, :, cut], gate.at[:, cut], sems_wide.at[2 * n]),
                pltpu.make_async_copy(up_any.at[0, :, cut], up.at[:, cut], sems_wide.at[2 * n + 1]),
            ]
        )
    tall = []
    for n, (at, size) in enumerate(pieces(down.shape[0], COLUMNS)):
        cut = pl.ds(at, size)
        tall.append([pltpu.make_async_copy(down_any.at[0, cut, :], down.at[cut, :], sems_down.at[n])])
    for copies in wide + tall:
        for copy in copies:
            copy.start()

    def ready(part, n):
        for copy in (wide, tall)[part][n]:
            copy.wait()

    expert_body(xa, xb, mask, gate, up, down, ya, yb, x, hidden, ready)


def expert_call(xa, xb, mask, weights, first=False):
    rows, width = xa.shape
    shapes = [w.shape[-2:] for w in weights]
    hidden, features = shapes[0][1], shapes[2][0]
    out = jax.ShapeDtypeStruct((rows, width), BF16)
    kept = tuple(pltpu.VMEM(shape, BF16) for shape in shapes) if first else ()
    place = pl.BlockSpec(memory_space=pltpu.VMEM)
    scratch = [pltpu.VMEM((2 * rows, width), BF16), pltpu.VMEM((2 * rows, hidden), BF16)]
    if first:
        scratch += [
            pltpu.SemaphoreType.DMA((2 * len(pieces(hidden, UNITS)),)),
            pltpu.SemaphoreType.DMA((len(pieces(features, COLUMNS)),)),
        ]
    weights = [pltpu.with_memory_space_constraint(w, pltpu.HBM if first else pltpu.VMEM) for w in weights]
    return pl.pallas_call(
        first_kernel if first else expert_kernel,
        out_shape=(out, out, *kept),
        in_specs=[place] * 3 + [pl.BlockSpec(memory_space=pl.ANY) if first else place] * 3,
        out_specs=(place,) * (2 + len(kept)),
        scratch_shapes=scratch,
        compiler_params=pltpu.CompilerParams(vmem_limit_bytes=16 * 2**20),
        cost_estimate=pl.CostEstimate(flops=0, bytes_accessed=0, transcendentals=0),
    )(xa, xb, mask, *weights)


def local_cube(tokens, norm_gain, expert_ids, gate_weights, gate_proj, up_proj, down_proj):
    tok_rows, features = tokens.shape
    devices = lax.axis_size("ex")
    experts = devices // SLICES
    mine = lax.axis_index("ex") % experts
    width = -(-(features + 3 * experts) // LANES) * LANES

    def swap(array, partner):
        return lax.ppermute(array, "ex", [(i, partner(i)) for i in range(devices)])

    def first(i):
        return i ^ (2 if i % 2 == 0 else 4)

    def second(i):
        return i ^ (4 if i % 2 == 0 else 2)

    def core(i):
        return i ^ 1

    def slice_bits(j):
        return lambda i: i ^ (j * experts)

    rows = rows_call(tokens, norm_gain, expert_ids, gate_weights, experts, width)
    lane = jnp.arange(LANES, dtype=jnp.int32)[None, :] - features % LANES
    ours = (lane >= 0) & (lane < 3 * experts) & (lane % experts == mine)
    mask = ours.astype(F32)
    weights = [gate_proj, up_proj, jnp.swapaxes(down_proj, 1, 2)]
    last = [mask]

    def order(value):
        value = lax.optimization_barrier((value, last[0]))[0]
        last[0] = value
        return value

    def expert(xa, xb):
        first_time = len(weights[0].shape) == 3
        parts = expert_call(xa, xb, mask, weights, first_time)
        if first_time:
            weights[:] = parts[2:]
        last[0] = parts[0]
        return parts[:2]

    def add(a, b):
        return (a.astype(F32) + b.astype(F32)).astype(BF16)

    p1, p2, half, ch, cp, near, far, back, q2, q1, z, zb = ([None] * SLICES for _ in range(12))

    def gather_half(j, block):
        half[j] = jnp.concatenate([block, order(p1[j])], axis=0)
        p2[j] = swap(half[j], second)
        ch[j] = swap(half[j], core)

    def gather_full(j):
        p2[j] = order(p2[j])
        cp[j] = swap(p2[j], core)

    def run_own(j):
        near[j], far[j] = expert(order(half[j]), p2[j])

    def run_other(j):
        mine_half = order(ch[j])
        back[j] = [swap(part, core) for part in expert(mine_half, order(cp[j]))]

    def reduce_core(j):
        q2[j] = swap(add(far[j], order(back[j][1])), second)

    def reduce_second(j):
        arrived = order(q2[j])
        near[j] = (near[j], order(back[j][0]), arrived)
        q1[j] = swap(total_of([a[tok_rows:] for a in near[j]]), first)

    def reduce_first(j):
        sums = total_of([a[:tok_rows] for a in near[j]] + [order(q1[j])])
        zb[j] = swap(sums, slice_bits(j)) if j else sums

    def total_of(arrays):
        return sum(a.astype(F32) for a in arrays).astype(BF16)

    p1[0] = order(swap(rows, first))
    z[1] = order(swap(rows, slice_bits(1)))
    z[2] = swap(order(rows), slice_bits(2))
    gather_half(0, rows)
    p1[1] = swap(z[1], first)
    gather_half(1, z[1])
    gather_full(0)
    run_own(0)
    z[2] = order(z[2])
    p1[2] = swap(z[2], first)
    z[3] = swap(order(rows), slice_bits(3))
    run_other(0)
    gather_half(2, z[2])
    gather_full(1)
    run_own(1)
    z[3] = order(z[3])
    p1[3] = swap(z[3], first)
    run_other(1)
    gather_half(3, z[3])
    gather_full(2)
    run_own(2)
    run_other(2)
    gather_full(3)
    reduce_core(1)
    reduce_core(2)
    run_own(3)
    run_other(3)
    reduce_second(1)
    reduce_second(2)
    reduce_core(3)
    reduce_first(1)
    reduce_first(2)
    reduce_core(0)
    reduce_second(3)
    zb[2] = order(zb[2])
    reduce_first(3)
    reduce_second(0)
    reduce_first(0)
    total = sum(order(zb[j]).astype(F32) for j in (2, 3, 1, 0))
    return total[:, :features].astype(BF16)


def solution(mesh):
    in_specs = (
        P(("groups", "ex"), None),
        P(),
        P(("groups", "ex"), None),
        P(("groups", "ex"), None),
        P("ex", None, None),
        P("ex", None, None),
        P("ex", None, None),
    )
    out_specs = P(("groups", "ex"), None)
    local = local_cube if mesh.shape["ex"] == 8 * SLICES else local_general
    return jax.shard_map(local, mesh=mesh, in_specs=in_specs, out_specs=out_specs, check_vma=False)
```

```python
import functools

import jax
import jax.numpy as jnp
from jax import lax
from jax.experimental import pallas as pl
from jax.experimental.pallas import tpu as pltpu
from jax.sharding import PartitionSpec as P

SLICES = 4
LANES = 128
UNITS = 2 * LANES
COLUMNS = 6 * LANES
BF16 = jnp.bfloat16
F32 = jnp.float32


def normalise(tokens, norm_gain):
    values = tokens.astype(F32)
    mean_sq = jnp.mean(values * values, axis=-1, keepdims=True)
    return (values * lax.rsqrt(mean_sq + 1e-05) * norm_gain).astype(BF16)


def expert_rows(flat_rows, gate_w, up_w, down_w):
    gate_act = jnp.dot(flat_rows, gate_w, preferred_element_type=F32)
    up_act = jnp.dot(flat_rows, up_w, preferred_element_type=F32)
    hidden = (jax.nn.silu(gate_act) * up_act).astype(BF16)
    return jnp.dot(hidden, down_w, preferred_element_type=F32)


def local_general(tokens, norm_gain, expert_ids, gate_weights, gate_proj, up_proj, down_proj):
    tok_rows, features = tokens.shape
    picks = expert_ids.shape[1]
    devices = lax.axis_size("ex")
    experts = devices // SLICES
    capacity = min(tok_rows, 4 * ((3 * tok_rows * picks + 8 * experts - 1) // (8 * experts)))
    normed = normalise(tokens, norm_gain)
    padded = jnp.concatenate([normed, jnp.zeros((1, features), normed.dtype)], axis=0)
    flat_expert = expert_ids.reshape(-1)
    onehot = (flat_expert[:, None] == jnp.arange(experts, dtype=jnp.int32)[None, :]).astype(
        jnp.int32
    )
    before = jnp.cumsum(onehot, axis=0) - onehot
    rank_in = jnp.sum(before * onehot, axis=1)
    token_index = jnp.arange(tok_rows * picks, dtype=jnp.int32) // picks
    slot_index = flat_expert * capacity + rank_in
    table = jnp.full((experts * capacity,), tok_rows, jnp.int32).at[slot_index].set(token_index)
    buffer = padded[table].reshape(experts, capacity, features)
    outgoing = jnp.tile(buffer, (SLICES, 1, 1))
    arrived = lax.all_to_all(outgoing, "ex", split_axis=0, concat_axis=0, tiled=True)
    partials = expert_rows(arrived.reshape(-1, features), gate_proj[0], up_proj[0], down_proj[0])
    partials = partials.reshape(devices, capacity, features)
    returned = lax.all_to_all(partials, "ex", split_axis=0, concat_axis=0, tiled=True)
    summed = jnp.sum(returned.reshape(SLICES, experts * capacity, features), axis=0)
    gathered = summed[slot_index].reshape(tok_rows, picks, features)
    mixed = jnp.sum(gathered * gate_weights[:, :, None], axis=1)
    return mixed.astype(BF16)


def pieces(extent, size):
    return [(at, min(size, extent - at)) for at in range(0, extent, size)]


def rows_kernel(
    experts, tokens_any, gain_any, ids_any, weights_any, rows_ref, tokens_ref, gain_ref, ids_ref, weights_ref, sems
):
    copies = [
        pltpu.make_async_copy(tokens_any, tokens_ref, sems.at[0]),
        pltpu.make_async_copy(gain_any, gain_ref, sems.at[1]),
        pltpu.make_async_copy(ids_any, ids_ref, sems.at[2]),
        pltpu.make_async_copy(weights_any, weights_ref, sems.at[3]),
    ]
    for copy in copies:
        copy.start()
    for copy in copies:
        copy.wait()
    tok_rows, features = tokens_ref.shape
    extra = rows_ref.shape[1] - features
    values = tokens_ref[...].astype(F32)
    mean_sq = jnp.sum(values * values, axis=-1, keepdims=True) * (1.0 / features)
    rows_ref[:, :features] = (values * lax.rsqrt(mean_sq + 1e-05) * gain_ref[...][None, :]).astype(BF16)
    place = lax.broadcasted_iota(jnp.int32, (extra, tok_rows), 0)
    expert = lax.rem(place, experts)
    dense = jnp.zeros((extra, tok_rows), F32)
    for j in range(ids_ref.shape[0]):
        dense += jnp.where(expert == ids_ref[j : j + 1, :], weights_ref[j : j + 1, :], 0.0)
    high = dense.astype(BF16).astype(F32)
    middle = (dense - high).astype(BF16).astype(F32)
    low = dense - high - middle
    term = jnp.where(place < experts, high, jnp.where(place < 2 * experts, middle, low))
    term = jnp.where(place < 3 * experts, term, 0.0).astype(BF16)
    row = lax.broadcasted_iota(jnp.int32, (extra, extra), 0)
    column = lax.broadcasted_iota(jnp.int32, (extra, extra), 1)
    unit = jnp.where(row == column, 1.0, 0.0).astype(BF16)
    turned = lax.dot_general(term, unit, (((0,), (0,)), ((), ())), preferred_element_type=F32)
    rows_ref[:, features:] = turned.astype(BF16)


def rows_call(tokens, norm_gain, expert_ids, gate_weights, experts, width):
    arrays = (tokens, norm_gain, jnp.swapaxes(expert_ids, 0, 1), jnp.swapaxes(gate_weights, 0, 1))
    return pl.pallas_call(
        functools.partial(rows_kernel, experts),
        out_shape=jax.ShapeDtypeStruct((tokens.shape[0], width), BF16),
        in_specs=[pl.BlockSpec(memory_space=pl.ANY)] * 4,
        out_specs=pl.BlockSpec(memory_space=pltpu.VMEM),
        scratch_shapes=[pltpu.VMEM(a.shape, a.dtype) for a in arrays] + [pltpu.SemaphoreType.DMA((4,))],
        compiler_params=pltpu.CompilerParams(vmem_limit_bytes=16 * 2**20),
    )(*(pltpu.with_memory_space_constraint(a, pltpu.HBM) for a in arrays))


def expert_body(xs, mask_ref, both_ref, down_ref, ys, x_ref, hidden_ref, ready):
    features, hidden = down_ref.shape
    at = 0
    for ref in xs:
        x_ref[at : at + ref.shape[0], :] = ref[...]
        at += ref.shape[0]
    for n, (at, size) in enumerate(pieces(hidden, UNITS)):
        ready(0, n)
        x = x_ref[:, :features]
        gate = jnp.dot(x, both_ref[:, 2 * at : 2 * at + size], preferred_element_type=F32)
        up = jnp.dot(x, both_ref[:, 2 * at + size : 2 * (at + size)], preferred_element_type=F32)
        hidden_ref[:, at : at + size] = (gate * jax.nn.sigmoid(gate) * up).astype(BF16)
    tail = features // LANES * LANES
    parts = x_ref[:, tail : tail + LANES].astype(F32)
    weight = jnp.sum(jnp.where(mask_ref[...] > 0.0, parts, 0.0), axis=1, keepdims=True)
    for n, (at, size) in enumerate(pieces(features, COLUMNS)):
        ready(1, n)
        y = lax.dot_general(
            hidden_ref[...],
            down_ref[at : at + size, :],
            (((1,), (1,)), ((), ())),
            preferred_element_type=F32,
        )
        y = (y * weight).astype(BF16)
        top = 0
        for ref in ys:
            ref[:, at : at + size] = y[top : top + ref.shape[0]]
            top += ref.shape[0]
    for ref in ys:
        ref[:, features:] = jnp.zeros((ref.shape[0], ref.shape[1] - features), BF16)


def expert_kernel(inputs, outputs, *refs):
    xs, (mask, both, down), refs = refs[:inputs], refs[inputs : inputs + 3], refs[inputs + 3 :]
    ys, (x, hidden) = refs[:outputs], refs[outputs:]
    expert_body(xs, mask, both, down, ys, x, hidden, lambda part, n: None)


def first_kernel(inputs, outputs, *refs):
    xs, (mask, gate, up, stored), refs = refs[:inputs], refs[inputs : inputs + 4], refs[inputs + 4 :]
    ys, (both, down, x, hidden, sems_wide, sems_down) = refs[:outputs], refs[outputs:]
    wide = []
    for n, (at, size) in enumerate(pieces(down.shape[1], UNITS)):
        cut = pl.ds(at, size)
        left, right = pl.ds(2 * at, size), pl.ds(2 * at + size, size)
        wide.append(
            [
                pltpu.make_async_copy(gate.at[0, :, cut], both.at[:, left], sems_wide.at[2 * n]),
                pltpu.make_async_copy(up.at[0, :, cut], both.at[:, right], sems_wide.at[2 * n + 1]),
            ]
        )
    tall = []
    for n, (at, size) in enumerate(pieces(down.shape[0], COLUMNS)):
        cut = pl.ds(at, size)
        tall.append([pltpu.make_async_copy(stored.at[0, cut, :], down.at[cut, :], sems_down.at[n])])
    for copies in wide + tall:
        for copy in copies:
            copy.start()

    def ready(part, n):
        for copy in (wide, tall)[part][n]:
            copy.wait()

    expert_body(xs, mask, both, down, ys, x, hidden, ready)


def expert_call(xs, mask, weights, splits, first=False):
    rows, width = sum(splits), xs[0].shape[1]
    features, hidden = weights[-1].shape[-2:]
    outs = tuple(jax.ShapeDtypeStruct((split, width), BF16) for split in splits)
    kept = (pltpu.VMEM((features, 2 * hidden), BF16), pltpu.VMEM((features, hidden), BF16)) if first else ()
    place = pl.BlockSpec(memory_space=pltpu.VMEM)
    scratch = [pltpu.VMEM((rows, width), BF16), pltpu.VMEM((rows, hidden), BF16)]
    if first:
        scratch += [
            pltpu.SemaphoreType.DMA((2 * len(pieces(hidden, UNITS)),)),
            pltpu.SemaphoreType.DMA((len(pieces(features, COLUMNS)),)),
        ]
    weights = [pltpu.with_memory_space_constraint(w, pltpu.HBM if first else pltpu.VMEM) for w in weights]
    stay = pl.BlockSpec(memory_space=pl.ANY) if first else place
    return pl.pallas_call(
        functools.partial(first_kernel if first else expert_kernel, len(xs), len(outs)),
        out_shape=(*outs, *kept),
        in_specs=[place] * (len(xs) + 1) + [stay] * len(weights),
        out_specs=(place,) * (len(outs) + len(kept)),
        scratch_shapes=scratch,
        compiler_params=pltpu.CompilerParams(vmem_limit_bytes=16 * 2**20),
        cost_estimate=pl.CostEstimate(flops=0, bytes_accessed=0, transcendentals=0),
    )(*xs, mask, *weights)


def local_cube(tokens, norm_gain, expert_ids, gate_weights, gate_proj, up_proj, down_proj):
    tok_rows, features = tokens.shape
    devices = lax.axis_size("ex")
    experts = devices // SLICES
    mine = lax.axis_index("ex") % experts
    width = -(-(features + 3 * experts) // LANES) * LANES

    def swap(array, partner):
        return lax.ppermute(array, "ex", [(i, partner(i)) for i in range(devices)])

    def first(i):
        return i ^ (2 if i % 2 == 0 else 4)

    def second(i):
        return i ^ (4 if i % 2 == 0 else 2)

    def core(i):
        return i ^ 1

    def slice_bits(j):
        return lambda i: i ^ (j * experts)

    def inner(array, outward):
        low = [(i, i - experts if outward else i + experts) for i in range(experts, 2 * experts)]
        high = [(i, i + experts if outward else i - experts) for i in range(2 * experts, 3 * experts)]
        return lax.ppermute(array, "ex", low + high)

    rows = rows_call(tokens, norm_gain, expert_ids, gate_weights, experts, width)
    lane = jnp.arange(LANES, dtype=jnp.int32)[None, :] - features % LANES
    ours = (lane >= 0) & (lane < 3 * experts) & (lane % experts == mine)
    mask = ours.astype(F32)
    weights = [gate_proj, up_proj, jnp.swapaxes(down_proj, 1, 2)]
    last = [mask]

    def order(value):
        value = lax.optimization_barrier((value, last[0]))[0]
        last[0] = value
        return value

    def expert(xs, splits):
        first_time = len(weights) == 3
        parts = expert_call(xs, mask, weights, splits, first_time)
        if first_time:
            weights[:] = parts[len(splits) :]
        last[0] = parts[0]
        return list(parts[: len(splits)])

    p1, p2, half, ch, cp, near, far, back, q2, q1, z, zb = ([None] * SLICES for _ in range(12))

    one, two = tok_rows, 2 * tok_rows

    def gather_half(j, block):
        p1[j] = order(p1[j])
        half[j] = jnp.concatenate([block, p1[j]], axis=0)
        p2[j] = swap(half[j], second)
        ch[j] = swap(half[j], core)

    def gather_full(j):
        p2[j] = order(p2[j])
        cp[j] = swap(p2[j], core)

    def run_early(j):
        near[j] = expert([order(half[j])], [one, one])

    def run_late(j):
        far[j] = expert([order(p2[j])], [two])[0]

    def run_own(j):
        *near[j], far[j] = expert([order(half[j]), p2[j]], [one, one, two])

    def run_other(j):
        mine_half = order(ch[j])
        back[j] = [swap(part, core) for part in expert([mine_half, order(cp[j])], [two, two])]

    def reduce_core(j):
        q2[j] = swap(total_of([far[j], order(back[j][1])]), second)

    def reduce_second(j):
        q2[j], back[j] = order(q2[j]), order(back[j][0])
        q1[j] = swap(total_of([near[j][1], back[j][one:], q2[j][one:]]), first)

    def reduce_first(j):
        sums = total_of([near[j][0], back[j][:one], q2[j][:one], order(q1[j])])
        zb[j] = swap(sums, slice_bits(j)) if j else sums

    def total_of(arrays):
        return sum(a.astype(F32) for a in arrays).astype(BF16)

    p1[0] = order(swap(rows, first))
    z[1] = order(swap(rows, slice_bits(1)))
    z[3] = order(inner(rows, False))
    z[2] = inner(z[1], False)
    outward = inner(z[3], True)
    gather_half(0, rows)
    p1[1] = swap(z[1], first)
    run_early(0)
    gather_half(1, z[1])
    gather_full(0)
    outward = order(outward)
    crossed = order(z[2])
    z[2] = crossed + outward
    p1[2] = swap(z[2], first)
    outward = inner(crossed, True)
    run_late(0)
    gather_half(2, z[2])
    gather_full(1)
    run_other(0)
    run_own(1)
    z[3] = z[3] + order(outward)
    p1[3] = swap(z[3], first)
    run_other(1)
    gather_half(3, z[3])
    gather_full(2)
    run_own(2)
    run_other(2)
    gather_full(3)
    reduce_core(1)
    reduce_core(2)
    run_own(3)
    run_other(3)
    reduce_second(1)
    reduce_second(2)
    reduce_core(3)
    reduce_first(1)
    reduce_first(2)
    reduce_core(0)
    reduce_second(3)
    zb[2] = order(zb[2])
    reduce_first(3)
    reduce_second(0)
    reduce_first(0)
    total = sum(order(zb[j]).astype(F32) for j in (2, 3, 1, 0))
    return total[:, :features].astype(BF16)


def solution(mesh):
    in_specs = (
        P(("groups", "ex"), None),
        P(),
        P(("groups", "ex"), None),
        P(("groups", "ex"), None),
        P("ex", None, None),
        P("ex", None, None),
        P("ex", None, None),
    )
    out_specs = P(("groups", "ex"), None)
    local = local_cube if mesh.shape["ex"] == 8 * SLICES else local_general
    return jax.shard_map(local, mesh=mesh, in_specs=in_specs, out_specs=out_specs, check_vma=False)
```

```python
import functools

import jax
import jax.numpy as jnp
from jax import lax
from jax.experimental import pallas as pl
from jax.experimental.pallas import tpu as pltpu
from jax.sharding import PartitionSpec as P

SLICES = 4
LANES = 128
UNITS = 2 * LANES
COLUMNS = 12 * LANES
BF16 = jnp.bfloat16
F32 = jnp.float32


def normalise(tokens, norm_gain):
    values = tokens.astype(F32)
    mean_sq = jnp.mean(values * values, axis=-1, keepdims=True)
    return (values * lax.rsqrt(mean_sq + 1e-05) * norm_gain).astype(BF16)


def expert_rows(flat_rows, gate_w, up_w, down_w):
    gate_act = jnp.dot(flat_rows, gate_w, preferred_element_type=F32)
    up_act = jnp.dot(flat_rows, up_w, preferred_element_type=F32)
    hidden = (jax.nn.silu(gate_act) * up_act).astype(BF16)
    return jnp.dot(hidden, down_w, preferred_element_type=F32)


def local_general(tokens, norm_gain, expert_ids, gate_weights, gate_proj, up_proj, down_proj):
    tok_rows, features = tokens.shape
    picks = expert_ids.shape[1]
    devices = lax.axis_size("ex")
    experts = devices // SLICES
    capacity = min(tok_rows, 4 * ((3 * tok_rows * picks + 8 * experts - 1) // (8 * experts)))
    normed = normalise(tokens, norm_gain)
    padded = jnp.concatenate([normed, jnp.zeros((1, features), normed.dtype)], axis=0)
    flat_expert = expert_ids.reshape(-1)
    onehot = (flat_expert[:, None] == jnp.arange(experts, dtype=jnp.int32)[None, :]).astype(
        jnp.int32
    )
    before = jnp.cumsum(onehot, axis=0) - onehot
    rank_in = jnp.sum(before * onehot, axis=1)
    token_index = jnp.arange(tok_rows * picks, dtype=jnp.int32) // picks
    slot_index = flat_expert * capacity + rank_in
    table = jnp.full((experts * capacity,), tok_rows, jnp.int32).at[slot_index].set(token_index)
    buffer = padded[table].reshape(experts, capacity, features)
    outgoing = jnp.tile(buffer, (SLICES, 1, 1))
    arrived = lax.all_to_all(outgoing, "ex", split_axis=0, concat_axis=0, tiled=True)
    partials = expert_rows(arrived.reshape(-1, features), gate_proj[0], up_proj[0], down_proj[0])
    partials = partials.reshape(devices, capacity, features)
    returned = lax.all_to_all(partials, "ex", split_axis=0, concat_axis=0, tiled=True)
    summed = jnp.sum(returned.reshape(SLICES, experts * capacity, features), axis=0)
    gathered = summed[slot_index].reshape(tok_rows, picks, features)
    mixed = jnp.sum(gathered * gate_weights[:, :, None], axis=1)
    return mixed.astype(BF16)


def pieces(extent, size):
    return [(at, min(size, extent - at)) for at in range(0, extent, size)]


def rows_kernel(
    experts, tokens_any, gain_any, ids_any, weights_any, rows_ref, tokens_ref, gain_ref, ids_ref, weights_ref, sems
):
    copies = [
        pltpu.make_async_copy(tokens_any, tokens_ref, sems.at[0]),
        pltpu.make_async_copy(gain_any, gain_ref, sems.at[1]),
        pltpu.make_async_copy(ids_any, ids_ref, sems.at[2]),
        pltpu.make_async_copy(weights_any, weights_ref, sems.at[3]),
    ]
    for copy in copies:
        copy.start()
    for copy in copies:
        copy.wait()
    tok_rows, features = tokens_ref.shape
    extra = rows_ref.shape[1] - features
    values = tokens_ref[...].astype(F32)
    mean_sq = jnp.sum(values * values, axis=-1, keepdims=True) * (1.0 / features)
    rows_ref[:, :features] = (values * lax.rsqrt(mean_sq + 1e-05) * gain_ref[...][None, :]).astype(BF16)
    place = lax.broadcasted_iota(jnp.int32, (extra, tok_rows), 0)
    expert = lax.rem(place, experts)
    dense = jnp.zeros((extra, tok_rows), F32)
    for j in range(ids_ref.shape[0]):
        dense += jnp.where(expert == ids_ref[j : j + 1, :], weights_ref[j : j + 1, :], 0.0)
    high = dense.astype(BF16).astype(F32)
    middle = (dense - high).astype(BF16).astype(F32)
    low = dense - high - middle
    term = jnp.where(place < experts, high, jnp.where(place < 2 * experts, middle, low))
    term = jnp.where(place < 3 * experts, term, 0.0).astype(BF16)
    row = lax.broadcasted_iota(jnp.int32, (extra, extra), 0)
    column = lax.broadcasted_iota(jnp.int32, (extra, extra), 1)
    unit = jnp.where(row == column, 1.0, 0.0).astype(BF16)
    turned = lax.dot_general(term, unit, (((0,), (0,)), ((), ())), preferred_element_type=F32)
    rows_ref[:, features:] = turned.astype(BF16)


def rows_call(tokens, norm_gain, expert_ids, gate_weights, experts, width):
    arrays = (tokens, norm_gain, jnp.swapaxes(expert_ids, 0, 1), jnp.swapaxes(gate_weights, 0, 1))
    return pl.pallas_call(
        functools.partial(rows_kernel, experts),
        out_shape=jax.ShapeDtypeStruct((tokens.shape[0], width), BF16),
        in_specs=[pl.BlockSpec(memory_space=pl.ANY)] * 4,
        out_specs=pl.BlockSpec(memory_space=pltpu.VMEM),
        scratch_shapes=[pltpu.VMEM(a.shape, a.dtype) for a in arrays] + [pltpu.SemaphoreType.DMA((4,))],
        compiler_params=pltpu.CompilerParams(vmem_limit_bytes=16 * 2**20),
    )(*(pltpu.with_memory_space_constraint(a, pltpu.HBM) for a in arrays))


def expert_body(xs, mask_ref, both_ref, down_ref, ys, x_ref, hidden_ref, ready):
    features, hidden = down_ref.shape
    at = 0
    for ref in xs:
        x_ref[at : at + ref.shape[0], :] = ref[...]
        at += ref.shape[0]
    for n, (at, size) in enumerate(pieces(hidden, UNITS)):
        ready(0, n)
        x = x_ref[:, :features]
        gate = jnp.dot(x, both_ref[:, 2 * at : 2 * at + size], preferred_element_type=F32)
        up = jnp.dot(x, both_ref[:, 2 * at + size : 2 * (at + size)], preferred_element_type=F32)
        hidden_ref[:, at : at + size] = (gate * jax.nn.sigmoid(gate) * up).astype(BF16)
    tail = features // LANES * LANES
    parts = x_ref[:, tail : tail + LANES].astype(F32)
    weight = jnp.sum(jnp.where(mask_ref[...] > 0.0, parts, 0.0), axis=1, keepdims=True)
    for n, (at, size) in enumerate(pieces(features, COLUMNS)):
        ready(1, n)
        y = lax.dot_general(
            hidden_ref[...],
            down_ref[at : at + size, :],
            (((1,), (1,)), ((), ())),
            preferred_element_type=F32,
        )
        y = (y * weight).astype(BF16)
        top = 0
        for ref in ys:
            ref[:, at : at + size] = y[top : top + ref.shape[0]]
            top += ref.shape[0]
    for ref in ys:
        ref[:, features:] = jnp.zeros((ref.shape[0], ref.shape[1] - features), BF16)


def expert_kernel(inputs, outputs, *refs):
    xs, (mask, both, down), refs = refs[:inputs], refs[inputs : inputs + 3], refs[inputs + 3 :]
    ys, (x, hidden) = refs[:outputs], refs[outputs:]
    expert_body(xs, mask, both, down, ys, x, hidden, lambda part, n: None)


def first_kernel(inputs, outputs, *refs):
    xs, (mask, gate, up, stored), refs = refs[:inputs], refs[inputs : inputs + 4], refs[inputs + 4 :]
    ys, (both, down, x, hidden, sems_wide, sems_down) = refs[:outputs], refs[outputs:]
    wide = []
    for n, (at, size) in enumerate(pieces(down.shape[1], UNITS)):
        cut = pl.ds(at, size)
        left, right = pl.ds(2 * at, size), pl.ds(2 * at + size, size)
        wide.append(
            [
                pltpu.make_async_copy(gate.at[0, :, cut], both.at[:, left], sems_wide.at[2 * n]),
                pltpu.make_async_copy(up.at[0, :, cut], both.at[:, right], sems_wide.at[2 * n + 1]),
            ]
        )
    tall = []
    for n, (at, size) in enumerate(pieces(down.shape[0], COLUMNS)):
        cut = pl.ds(at, size)
        tall.append([pltpu.make_async_copy(stored.at[0, cut, :], down.at[cut, :], sems_down.at[n])])
    for copies in wide + tall:
        for copy in copies:
            copy.start()

    def ready(part, n):
        for copy in (wide, tall)[part][n]:
            copy.wait()

    expert_body(xs, mask, both, down, ys, x, hidden, ready)


def expert_call(xs, mask, weights, splits, first=False):
    rows, width = sum(splits), xs[0].shape[1]
    features, hidden = weights[-1].shape[-2:]
    outs = tuple(jax.ShapeDtypeStruct((split, width), BF16) for split in splits)
    kept = (pltpu.VMEM((features, 2 * hidden), BF16), pltpu.VMEM((features, hidden), BF16)) if first else ()
    place = pl.BlockSpec(memory_space=pltpu.VMEM)
    scratch = [pltpu.VMEM((rows, width), BF16), pltpu.VMEM((rows, hidden), BF16)]
    if first:
        scratch += [
            pltpu.SemaphoreType.DMA((2 * len(pieces(hidden, UNITS)),)),
            pltpu.SemaphoreType.DMA((len(pieces(features, COLUMNS)),)),
        ]
    weights = [pltpu.with_memory_space_constraint(w, pltpu.HBM if first else pltpu.VMEM) for w in weights]
    stay = pl.BlockSpec(memory_space=pl.ANY) if first else place
    return pl.pallas_call(
        functools.partial(first_kernel if first else expert_kernel, len(xs), len(outs)),
        out_shape=(*outs, *kept),
        in_specs=[place] * (len(xs) + 1) + [stay] * len(weights),
        out_specs=(place,) * (len(outs) + len(kept)),
        scratch_shapes=scratch,
        compiler_params=pltpu.CompilerParams(vmem_limit_bytes=16 * 2**20),
        cost_estimate=pl.CostEstimate(flops=0, bytes_accessed=0, transcendentals=0),
    )(*xs, mask, *weights)


def local_cube(tokens, norm_gain, expert_ids, gate_weights, gate_proj, up_proj, down_proj):
    tok_rows, features = tokens.shape
    devices = lax.axis_size("ex")
    experts = devices // SLICES
    mine = lax.axis_index("ex") % experts
    width = -(-(features + 3 * experts) // LANES) * LANES

    def swap(array, partner):
        return lax.ppermute(array, "ex", [(i, partner(i)) for i in range(devices)])

    def first(i):
        return i ^ (2 if i % 2 == 0 else 4)

    def second(i):
        return i ^ (4 if i % 2 == 0 else 2)

    def core(i):
        return i ^ 1

    def slice_bits(j):
        return lambda i: i ^ (j * experts)

    def inner(array, outward):
        low = [(i, i - experts if outward else i + experts) for i in range(experts, 2 * experts)]
        high = [(i, i + experts if outward else i - experts) for i in range(2 * experts, 3 * experts)]
        return lax.ppermute(array, "ex", low + high)

    rows = rows_call(tokens, norm_gain, expert_ids, gate_weights, experts, width)
    lane = jnp.arange(LANES, dtype=jnp.int32)[None, :] - features % LANES
    ours = (lane >= 0) & (lane < 3 * experts) & (lane % experts == mine)
    mask = ours.astype(F32)
    weights = [gate_proj, up_proj, jnp.swapaxes(down_proj, 1, 2)]
    last = [mask]

    def order(value):
        value = lax.optimization_barrier((value, last[0]))[0]
        last[0] = value
        return value

    def expert(xs, splits):
        first_time = len(weights) == 3
        parts = expert_call(xs, mask, weights, splits, first_time)
        if first_time:
            weights[:] = parts[len(splits) :]
        last[0] = parts[0]
        return list(parts[: len(splits)])

    p1, p2, half, ch, cp, near, far, back, q2, q1, z, zb = ([None] * SLICES for _ in range(12))

    one, two = tok_rows, 2 * tok_rows

    def gather_half(j, block):
        p1[j] = order(p1[j])
        half[j] = jnp.concatenate([block, p1[j]], axis=0)
        p2[j] = swap(half[j], second)
        ch[j] = swap(half[j], core)

    def gather_full(j):
        p2[j] = order(p2[j])
        cp[j] = swap(p2[j], core)

    def run_early(j):
        near[j] = expert([order(half[j])], [one, one])

    def run_late(j):
        far[j] = expert([order(p2[j])], [two])[0]

    def run_own(j):
        *near[j], far[j] = expert([order(half[j]), p2[j]], [one, one, two])

    def run_other(j):
        mine_half = order(ch[j])
        back[j] = [swap(part, core) for part in expert([mine_half, order(cp[j])], [two, two])]

    def reduce_core(j):
        q2[j] = swap(total_of([far[j], order(back[j][1])]), second)

    def reduce_second(j):
        q2[j], back[j] = order(q2[j]), order(back[j][0])
        q1[j] = swap(total_of([near[j][1], back[j][one:], q2[j][one:]]), first)

    def reduce_first(j):
        sums = total_of([near[j][0], back[j][:one], q2[j][:one], order(q1[j])])
        zb[j] = swap(sums, slice_bits(j)) if j else sums

    def total_of(arrays):
        return sum(a.astype(F32) for a in arrays).astype(BF16)

    p1[0] = order(swap(rows, first))
    z[1] = order(swap(rows, slice_bits(1)))
    z[3] = order(inner(rows, False))
    z[2] = inner(z[1], False)
    outward = inner(z[3], True)
    gather_half(0, rows)
    p1[1] = swap(z[1], first)
    run_early(0)
    gather_half(1, z[1])
    gather_full(0)
    outward = order(outward)
    crossed = order(z[2])
    z[2] = crossed + outward
    p1[2] = swap(z[2], first)
    outward = inner(crossed, True)
    run_late(0)
    gather_full(1)
    z[3] = z[3] + order(outward)
    p1[3] = swap(z[3], first)
    gather_half(2, z[2])
    run_other(0)
    run_own(1)
    run_other(1)
    gather_half(3, z[3])
    gather_full(2)
    run_own(2)
    run_other(2)
    gather_full(3)
    reduce_core(1)
    reduce_core(2)
    run_own(3)
    run_other(3)
    reduce_second(1)
    reduce_second(2)
    reduce_core(3)
    reduce_first(1)
    reduce_first(2)
    reduce_core(0)
    reduce_second(3)
    zb[2] = order(zb[2])
    reduce_first(3)
    reduce_second(0)
    reduce_first(0)
    total = sum(order(zb[j]).astype(F32) for j in (2, 3, 1, 0))
    return total[:, :features].astype(BF16)


def solution(mesh):
    in_specs = (
        P(("groups", "ex"), None),
        P(),
        P(("groups", "ex"), None),
        P(("groups", "ex"), None),
        P("ex", None, None),
        P("ex", None, None),
        P("ex", None, None),
    )
    out_specs = P(("groups", "ex"), None)
    local = local_cube if mesh.shape["ex"] == 8 * SLICES else local_general
    return jax.shard_map(local, mesh=mesh, in_specs=in_specs, out_specs=out_specs, check_vma=False)
```

```python
import functools

import jax
import jax.numpy as jnp
from jax import lax
from jax.experimental import pallas as pl
from jax.experimental.pallas import tpu as pltpu
from jax.sharding import PartitionSpec as P

SLICES = 4
LANES = 128
UNITS = 2 * LANES
COLUMNS = 23 * LANES
BF16 = jnp.bfloat16
F32 = jnp.float32


def normalise(tokens, norm_gain):
    values = tokens.astype(F32)
    mean_sq = jnp.mean(values * values, axis=-1, keepdims=True)
    return (values * lax.rsqrt(mean_sq + 1e-05) * norm_gain).astype(BF16)


def expert_rows(flat_rows, gate_w, up_w, down_w):
    gate_act = jnp.dot(flat_rows, gate_w, preferred_element_type=F32)
    up_act = jnp.dot(flat_rows, up_w, preferred_element_type=F32)
    hidden = (jax.nn.silu(gate_act) * up_act).astype(BF16)
    return jnp.dot(hidden, down_w, preferred_element_type=F32)


def local_general(tokens, norm_gain, expert_ids, gate_weights, gate_proj, up_proj, down_proj):
    tok_rows, features = tokens.shape
    picks = expert_ids.shape[1]
    devices = lax.axis_size("ex")
    experts = devices // SLICES
    capacity = min(tok_rows, 4 * ((3 * tok_rows * picks + 8 * experts - 1) // (8 * experts)))
    normed = normalise(tokens, norm_gain)
    padded = jnp.concatenate([normed, jnp.zeros((1, features), normed.dtype)], axis=0)
    flat_expert = expert_ids.reshape(-1)
    onehot = (flat_expert[:, None] == jnp.arange(experts, dtype=jnp.int32)[None, :]).astype(
        jnp.int32
    )
    before = jnp.cumsum(onehot, axis=0) - onehot
    rank_in = jnp.sum(before * onehot, axis=1)
    token_index = jnp.arange(tok_rows * picks, dtype=jnp.int32) // picks
    slot_index = flat_expert * capacity + rank_in
    table = jnp.full((experts * capacity,), tok_rows, jnp.int32).at[slot_index].set(token_index)
    buffer = padded[table].reshape(experts, capacity, features)
    outgoing = jnp.tile(buffer, (SLICES, 1, 1))
    arrived = lax.all_to_all(outgoing, "ex", split_axis=0, concat_axis=0, tiled=True)
    partials = expert_rows(arrived.reshape(-1, features), gate_proj[0], up_proj[0], down_proj[0])
    partials = partials.reshape(devices, capacity, features)
    returned = lax.all_to_all(partials, "ex", split_axis=0, concat_axis=0, tiled=True)
    summed = jnp.sum(returned.reshape(SLICES, experts * capacity, features), axis=0)
    gathered = summed[slot_index].reshape(tok_rows, picks, features)
    mixed = jnp.sum(gathered * gate_weights[:, :, None], axis=1)
    return mixed.astype(BF16)


def pieces(extent, size):
    return [(at, min(size, extent - at)) for at in range(0, extent, size)]


def rows_kernel(
    experts, tokens_any, gain_any, ids_any, weights_any, rows_ref, tokens_ref, gain_ref, ids_ref, weights_ref, sems
):
    copies = [
        pltpu.make_async_copy(tokens_any, tokens_ref, sems.at[0]),
        pltpu.make_async_copy(gain_any, gain_ref, sems.at[1]),
        pltpu.make_async_copy(ids_any, ids_ref, sems.at[2]),
        pltpu.make_async_copy(weights_any, weights_ref, sems.at[3]),
    ]
    for copy in copies:
        copy.start()
    for copy in copies:
        copy.wait()
    tok_rows, features = tokens_ref.shape
    extra = rows_ref.shape[1] - features
    values = tokens_ref[...].astype(F32)
    mean_sq = jnp.sum(values * values, axis=-1, keepdims=True) * (1.0 / features)
    rows_ref[:, :features] = (values * lax.rsqrt(mean_sq + 1e-05) * gain_ref[...][None, :]).astype(BF16)
    place = lax.broadcasted_iota(jnp.int32, (extra, tok_rows), 0)
    expert = lax.rem(place, experts)
    dense = jnp.zeros((extra, tok_rows), F32)
    for j in range(ids_ref.shape[0]):
        dense += jnp.where(expert == ids_ref[j : j + 1, :], weights_ref[j : j + 1, :], 0.0)
    high = dense.astype(BF16).astype(F32)
    middle = (dense - high).astype(BF16).astype(F32)
    low = dense - high - middle
    term = jnp.where(place < experts, high, jnp.where(place < 2 * experts, middle, low))
    term = jnp.where(place < 3 * experts, term, 0.0).astype(BF16)
    row = lax.broadcasted_iota(jnp.int32, (extra, extra), 0)
    column = lax.broadcasted_iota(jnp.int32, (extra, extra), 1)
    unit = jnp.where(row == column, 1.0, 0.0).astype(BF16)
    turned = lax.dot_general(term, unit, (((0,), (0,)), ((), ())), preferred_element_type=F32)
    rows_ref[:, features:] = turned.astype(BF16)


def rows_call(tokens, norm_gain, expert_ids, gate_weights, experts, width):
    arrays = (tokens, norm_gain, jnp.swapaxes(expert_ids, 0, 1), jnp.swapaxes(gate_weights, 0, 1))
    return pl.pallas_call(
        functools.partial(rows_kernel, experts),
        out_shape=jax.ShapeDtypeStruct((tokens.shape[0], width), BF16),
        in_specs=[pl.BlockSpec(memory_space=pl.ANY)] * 4,
        out_specs=pl.BlockSpec(memory_space=pltpu.VMEM),
        scratch_shapes=[pltpu.VMEM(a.shape, a.dtype) for a in arrays] + [pltpu.SemaphoreType.DMA((4,))],
        compiler_params=pltpu.CompilerParams(vmem_limit_bytes=16 * 2**20),
    )(*(pltpu.with_memory_space_constraint(a, pltpu.HBM) for a in arrays))


def expert_body(xs, mask_ref, both_ref, down_ref, ys, x_ref, hidden_ref, ready):
    features, hidden = down_ref.shape
    at = 0
    for ref in xs:
        x_ref[at : at + ref.shape[0], :] = ref[...]
        at += ref.shape[0]
    for n, (at, size) in enumerate(pieces(hidden, UNITS)):
        ready(0, n)
        x = x_ref[:, :features]
        gate = jnp.dot(x, both_ref[:, 2 * at : 2 * at + size], preferred_element_type=F32)
        up = jnp.dot(x, both_ref[:, 2 * at + size : 2 * (at + size)], preferred_element_type=F32)
        hidden_ref[:, at : at + size] = (gate * jax.nn.sigmoid(gate) * up).astype(BF16)
    tail = features // LANES * LANES
    parts = x_ref[:, tail : tail + LANES].astype(F32)
    weight = jnp.sum(jnp.where(mask_ref[...] > 0.0, parts, 0.0), axis=1, keepdims=True)
    for n, (at, size) in enumerate(pieces(features, COLUMNS)):
        ready(1, n)
        y = lax.dot_general(
            hidden_ref[...],
            down_ref[at : at + size, :],
            (((1,), (1,)), ((), ())),
            preferred_element_type=F32,
        )
        y = (y * weight).astype(BF16)
        top = 0
        for ref in ys:
            ref[:, at : at + size] = y[top : top + ref.shape[0]]
            top += ref.shape[0]
    for ref in ys:
        ref[:, features:] = jnp.zeros((ref.shape[0], ref.shape[1] - features), BF16)


def expert_kernel(inputs, outputs, *refs):
    xs, (mask, both, down), refs = refs[:inputs], refs[inputs : inputs + 3], refs[inputs + 3 :]
    ys, (x, hidden) = refs[:outputs], refs[outputs:]
    expert_body(xs, mask, both, down, ys, x, hidden, lambda part, n: None)


def first_kernel(inputs, outputs, *refs):
    xs, (mask, gate, up, stored), refs = refs[:inputs], refs[inputs : inputs + 4], refs[inputs + 4 :]
    ys, (both, down, x, hidden, sems_wide, sems_down) = refs[:outputs], refs[outputs:]
    wide = []
    for n, (at, size) in enumerate(pieces(down.shape[1], UNITS)):
        cut = pl.ds(at, size)
        left, right = pl.ds(2 * at, size), pl.ds(2 * at + size, size)
        wide.append(
            [
                pltpu.make_async_copy(gate.at[0, :, cut], both.at[:, left], sems_wide.at[2 * n]),
                pltpu.make_async_copy(up.at[0, :, cut], both.at[:, right], sems_wide.at[2 * n + 1]),
            ]
        )
    tall = []
    for n, (at, size) in enumerate(pieces(down.shape[0], COLUMNS)):
        cut = pl.ds(at, size)
        tall.append([pltpu.make_async_copy(stored.at[0, cut, :], down.at[cut, :], sems_down.at[n])])
    for copies in wide + tall:
        for copy in copies:
            copy.start()

    def ready(part, n):
        for copy in (wide, tall)[part][n]:
            copy.wait()

    expert_body(xs, mask, both, down, ys, x, hidden, ready)


def expert_call(xs, mask, weights, splits, first=False):
    rows, width = sum(splits), xs[0].shape[1]
    features, hidden = weights[-1].shape[-2:]
    outs = tuple(jax.ShapeDtypeStruct((split, width), BF16) for split in splits)
    kept = (pltpu.VMEM((features, 2 * hidden), BF16), pltpu.VMEM((features, hidden), BF16)) if first else ()
    place = pl.BlockSpec(memory_space=pltpu.VMEM)
    scratch = [pltpu.VMEM((rows, width), BF16), pltpu.VMEM((rows, hidden), BF16)]
    if first:
        scratch += [
            pltpu.SemaphoreType.DMA((2 * len(pieces(hidden, UNITS)),)),
            pltpu.SemaphoreType.DMA((len(pieces(features, COLUMNS)),)),
        ]
    weights = [pltpu.with_memory_space_constraint(w, pltpu.HBM if first else pltpu.VMEM) for w in weights]
    stay = pl.BlockSpec(memory_space=pl.ANY) if first else place
    return pl.pallas_call(
        functools.partial(first_kernel if first else expert_kernel, len(xs), len(outs)),
        out_shape=(*outs, *kept),
        in_specs=[place] * (len(xs) + 1) + [stay] * len(weights),
        out_specs=(place,) * (len(outs) + len(kept)),
        scratch_shapes=scratch,
        compiler_params=pltpu.CompilerParams(vmem_limit_bytes=16 * 2**20),
        cost_estimate=pl.CostEstimate(flops=0, bytes_accessed=0, transcendentals=0),
    )(*xs, mask, *weights)


def local_cube(tokens, norm_gain, expert_ids, gate_weights, gate_proj, up_proj, down_proj):
    tok_rows, features = tokens.shape
    devices = lax.axis_size("ex")
    experts = devices // SLICES
    mine = lax.axis_index("ex") % experts
    width = -(-(features + 3 * experts) // LANES) * LANES

    def swap(array, partner):
        return lax.ppermute(array, "ex", [(i, partner(i)) for i in range(devices)])

    def first(i):
        return i ^ (2 if i % 2 == 0 else 4)

    def second(i):
        return i ^ (4 if i % 2 == 0 else 2)

    def core(i):
        return i ^ 1

    def slice_bits(j):
        return lambda i: i ^ (j * experts)

    def inner(array, outward):
        low = [(i, i - experts if outward else i + experts) for i in range(experts, 2 * experts)]
        high = [(i, i + experts if outward else i - experts) for i in range(2 * experts, 3 * experts)]
        return lax.ppermute(array, "ex", low + high)

    rows = rows_call(tokens, norm_gain, expert_ids, gate_weights, experts, width)
    lane = jnp.arange(LANES, dtype=jnp.int32)[None, :] - features % LANES
    ours = (lane >= 0) & (lane < 3 * experts) & (lane % experts == mine)
    mask = ours.astype(F32)
    weights = [gate_proj, up_proj, jnp.swapaxes(down_proj, 1, 2)]
    last = [mask]

    def order(value):
        value = lax.optimization_barrier((value, last[0]))[0]
        last[0] = value
        return value

    def expert(xs, splits):
        first_time = len(weights) == 3
        parts = expert_call(xs, mask, weights, splits, first_time)
        if first_time:
            weights[:] = parts[len(splits) :]
        last[0] = parts[0]
        return list(parts[: len(splits)])

    p1, p2, half, ch, cp, near, far, back, q2, q1, z, zb = ([None] * SLICES for _ in range(12))

    one, two = tok_rows, 2 * tok_rows

    def gather_half(j, block):
        p1[j] = order(p1[j])
        half[j] = jnp.concatenate([block, p1[j]], axis=0)
        p2[j] = swap(half[j], second)
        ch[j] = swap(half[j], core)

    def gather_full(j):
        p2[j] = order(p2[j])
        cp[j] = swap(p2[j], core)

    def run_early(j):
        near[j] = expert([order(half[j])], [one, one])

    def run_late(j):
        far[j] = expert([order(p2[j])], [two])[0]

    def run_own(j):
        *near[j], far[j] = expert([order(half[j]), p2[j]], [one, one, two])

    def run_other(j):
        mine_half = order(ch[j])
        back[j] = [swap(part, core) for part in expert([mine_half, order(cp[j])], [two, two])]

    def reduce_core(j):
        q2[j] = swap(total_of([far[j], order(back[j][1])]), second)

    def reduce_second(j):
        q2[j], back[j] = order(q2[j]), order(back[j][0])
        q1[j] = swap(total_of([near[j][1], back[j][one:], q2[j][one:]]), first)

    def reduce_first(j):
        sums = total_of([near[j][0], back[j][:one], q2[j][:one], order(q1[j])])
        zb[j] = swap(sums, slice_bits(j)) if j else sums

    def total_of(arrays):
        return sum(a.astype(F32) for a in arrays).astype(BF16)

    p1[0] = order(swap(rows, first))
    z[1] = order(swap(rows, slice_bits(1)))
    z[3] = order(inner(rows, False))
    z[2] = inner(z[1], False)
    outward = inner(z[3], True)
    gather_half(0, rows)
    p1[1] = swap(z[1], first)
    run_early(0)
    gather_half(1, z[1])
    gather_full(0)
    outward = order(outward)
    crossed = order(z[2])
    z[2] = crossed + outward
    p1[2] = swap(z[2], first)
    outward = inner(crossed, True)
    run_late(0)
    gather_full(1)
    z[3] = z[3] + order(outward)
    p1[3] = swap(z[3], first)
    gather_half(2, z[2])
    run_other(0)
    run_own(1)
    run_other(1)
    gather_half(3, z[3])
    gather_full(2)
    run_own(2)
    run_other(2)
    gather_full(3)
    reduce_core(1)
    reduce_core(2)
    run_own(3)
    run_other(3)
    reduce_second(1)
    reduce_second(2)
    reduce_core(3)
    reduce_first(1)
    reduce_first(2)
    reduce_core(0)
    reduce_second(3)
    zb[2] = order(zb[2])
    reduce_first(3)
    reduce_second(0)
    reduce_first(0)
    total = sum(order(zb[j]).astype(F32) for j in (2, 3, 1, 0))
    return total[:, :features].astype(BF16)


def solution(mesh):
    in_specs = (
        P(("groups", "ex"), None),
        P(),
        P(("groups", "ex"), None),
        P(("groups", "ex"), None),
        P("ex", None, None),
        P("ex", None, None),
        P("ex", None, None),
    )
    out_specs = P(("groups", "ex"), None)
    local = local_cube if mesh.shape["ex"] == 8 * SLICES else local_general
    return jax.shard_map(local, mesh=mesh, in_specs=in_specs, out_specs=out_specs, check_vma=False)
```
